512 devices in a mesh: segment: 16 (over x, y), width: 32 (over z, core).
Axes of the slice: x: 4, y: 4, z: 16, core: 2. Of those that a mesh axis runs over, the one named last changes fastest.
Arguments:
- samples: bfloat16 [32, 65536], P(None, 'width'), may hold values from -6 to 6
- occupancy: int32 [16, 512, 4], P('segment'), may hold values from 0 to 511, as said below
- weights: bfloat16 [16, 512, 4, 128, 128], P('segment', 'width'), may hold values from -0.375 to 0.375
- biases: float32 [16, 65536], P('segment', 'width'), may hold values from -3 to 3
Outputs:
- final: bfloat16 [32, 65536], P('segment', 'width')
The draws below stay inside these ranges and needn't reach their ends.
Inputs may be any that keep to these rules, and one draw needn't show every extreme that they name: `occupancy`: for each layer and width index d, the 16 column blocks d*16 to (d+1)*16 - 1 each name 4 different row blocks; together they name 32 different row blocks, each by exactly 2 of them, at most 2 in any one range e*16 to (e+1)*16 - 1, and exactly 2 in some ranges.
All inputs are finite; a program needn't handle non-finite values.
Results may differ from the reference program's by a relative error of at most 0.025.
Values may be sent and summed in bfloat16 or wider, within the bound.
A program may use at most 64 MiB of HBM per device.

```python
import jax
import jax.numpy as jnp

N = 65536
BS = 128
K = 4
LAYERS = 16
NB = 512
BLK_DEV = 16
CAP = 2
ROWS = 32


def draw_occupancy(key, part):
    key = jax.random.fold_in(key, 7)
    shards = NB // BLK_DEV
    pool_size = 2 * BLK_DEV
    quarter = shards // 4
    pattern = jnp.concatenate([jnp.full((quarter,), CAP, jnp.int32), jnp.full((shards - 2 * quarter,), CAP // 2, jnp.int32), jnp.zeros((quarter,), jnp.int32)])

    def one_group(subkey):
        first, second, third = jax.random.split(subkey, 3)
        counts = jax.random.permutation(first, pattern)
        local = jax.vmap(lambda inner: jax.random.permutation(inner, BLK_DEV)[:CAP])(jax.random.split(second, shards))
        candidate = (jnp.arange(shards, dtype=jnp.int32)[:, None] * BLK_DEV + local).reshape(-1)
        valid = (jnp.arange(CAP, dtype=jnp.int32)[None, :] < counts[:, None]).reshape(-1)
        score = jnp.where(valid, 0, shards * CAP) + jnp.arange(shards * CAP, dtype=jnp.int32)
        chosen = jnp.argsort(score)[:pool_size]
        pool = candidate[chosen]
        mixed = pool[jax.random.permutation(third, pool_size)]
        column = jnp.arange(BLK_DEV, dtype=jnp.int32)
        return jnp.stack([mixed[2 * column], mixed[2 * column + 1], mixed[(2 * column + BLK_DEV) % pool_size], mixed[(2 * column + 1 + BLK_DEV) % pool_size]], axis=1)
    groups = jax.vmap(one_group)(jax.random.split(key, LAYERS * shards))
    return groups.reshape(LAYERS, NB, 4).astype(jnp.int32)


def steps_of(stream_key, shape, cuts, low, top_value):
    factor_of, own = 1.0, jax.random.fold_in(stream_key, 6)
    for axis_at, shards_of in cuts:
        steps = jnp.exp(jax.random.uniform(jax.random.fold_in(own, axis_at), (shards_of,), jnp.float32, low / len(cuts), top_value / len(cuts)))
        factor_of = factor_of * jnp.repeat(steps, shape[axis_at] // shards_of).reshape([-1 if axis == axis_at else 1 for axis in range(len(shape))])
    return factor_of


def scatter_about(rng, dims, spread, limit, cuts=(), kind=jnp.bfloat16):
    entries = jax.random.normal(rng, dims, jnp.float32) * spread
    if len(cuts) > 0:
        entries = steps_of(rng, dims, cuts, -0.22, 0.18) * entries
    return jnp.clip(entries, min=-limit, max=limit).astype(kind)


def setup_inputs(seed: int = 0) -> dict:
    key_list = jax.random.split(jax.random.key(seed), 5)
    samples = scatter_about(key_list[0], (ROWS, N), 1.0, 6.0, ((1, 32),))
    occupancy = draw_occupancy(jax.random.fold_in(key_list[4], 71), 0)
    weights = scatter_about(key_list[2], (LAYERS, NB, K, BS, BS), (K * BS // 2) ** -0.5, 0.375, ((0, 16), (1, 32)))
    biases = scatter_about(key_list[3], (LAYERS, N), 0.5, 3.0, ((0, 16), (1, 32)), jnp.float32)
    return {"samples": samples, "occupancy": occupancy, "weights": weights, "biases": biases}


def reference(samples, occupancy, weights, biases):
    rows = samples.shape[0]
    act = samples
    for layer in range(LAYERS):
        pieces = act.reshape(rows, NB, BS)
        picked = jnp.take(pieces, occupancy[layer].reshape(-1), axis=1).reshape(rows, NB, K, BS)
        pre = jnp.einsum("rcki,ckio->rco", picked.astype(jnp.float32), weights[layer].astype(jnp.float32))
        pre = pre + biases[layer].reshape(1, NB, BS)
        act = jnp.clip(pre, 0.0, 4.0).astype(jnp.bfloat16).reshape(rows, N)
    return act
```

```python
import functools

import jax
import jax.numpy as jnp
from jax import lax
from jax.experimental import pallas as pl
from jax.experimental.pallas import tpu as pltpu
from jax.sharding import PartitionSpec as P

BATCH = 8
CLIP = 4.0
SLOTS = 2
MESH = pl.DeviceIdType.MESH


def kernel(
    tab_ref, idx_ref, samples_ref, weights_ref, bias_ref, out_ref,
    w, recv, send, stage, act, first, fin, got,
    w_sem, send_sem, recv_sem, fin_sem, got_sem,
):
    segments, shards = lax.axis_size("segment"), lax.axis_size("width")
    seg, me = lax.axis_index("segment"), lax.axis_index("width")
    after = lax.rem(seg + 1, segments)
    before = lax.rem(seg + segments - 1, segments)
    last = segments - 1
    micro, owned, batch, order = first.shape
    per_col = w.shape[1] // order
    share = got.shape[0]
    pairs = batch // share

    load_w = pltpu.make_async_copy(weights_ref, w, w_sem)
    load_w.start()

    barrier = pltpu.get_barrier_semaphore()
    for e in range(shards):
        pl.semaphore_signal(barrier, inc=1, device_id=(before, e), device_id_type=MESH)

    @pl.when(seg != last)
    def _():
        pl.semaphore_signal(barrier, inc=1, device_id=(last, me), device_id_type=MESH)

    pl.semaphore_wait(barrier, jnp.where(seg == last, shards + last, shards))

    offsets = sorted(range(shards), key=lambda o: -min(o, shards - o))

    def emit(m, block):
        for off in offsets:
            d = lax.rem(me + off, shards)
            parts = [block(tab_ref[d * SLOTS + j]) for j in range(SLOTS)]
            send[m, d] = jnp.concatenate(parts, axis=0).astype(jnp.bfloat16)
            pltpu.make_async_remote_copy(
                src_ref=send.at[m, d],
                dst_ref=recv.at[m, me],
                send_sem=send_sem.at[m],
                recv_sem=recv_sem.at[m],
                device_id=(after, d),
                device_id_type=MESH,
            ).start()

    @pl.when(seg == last)
    def _():
        rows = samples_ref.shape[0]
        for c in range(owned):
            block = samples_ref[:, c * order:(c + 1) * order].astype(jnp.float32)
            for m in range(rows // batch):
                first[m, c] = block[m * batch:(m + 1) * batch]

        @pl.loop(0, micro)
        def _(m):
            emit(m, lambda i: first[m, i])

    load_w.wait()

    @pl.loop(0, micro)
    def _(m):
        pltpu.make_async_copy(recv.at[m], recv.at[m], recv_sem.at[m]).wait()
        for e in range(shards):
            both = recv[m, e].astype(jnp.float32)
            for j in range(SLOTS):
                stage[e * SLOTS + j] = both[j * batch:(j + 1) * batch]
        for c in range(owned):
            named = [stage[idx_ref[c * per_col + k]] for k in range(per_col)]
            named = jnp.concatenate(named, axis=1).astype(jnp.bfloat16)
            pre = jnp.dot(named, w[c], preferred_element_type=jnp.float32)
            pre = pre + bias_ref[0:1, c * order:(c + 1) * order]
            act[c] = jnp.clip(pre, 0.0, CLIP)

        @pl.when(seg != last)
        def _():
            emit(m, lambda i: act[i])

        @pl.when(seg == last)
        def _():
            for j in range(pairs):
                for c in range(owned):
                    fin[m, j, :, c * order:(c + 1) * order] = act[
                        c, j * share:(j + 1) * share, :
                    ].astype(jnp.bfloat16)
                owner = m * pairs + j

                @pl.when(owner != last)
                def _():
                    pltpu.make_async_remote_copy(
                        src_ref=fin.at[m, j],
                        dst_ref=got,
                        send_sem=fin_sem,
                        recv_sem=got_sem,
                        device_id=(owner, me),
                        device_id_type=MESH,
                    ).start()

    @pl.loop(0, micro)
    def _(m):
        pltpu.make_async_copy(send.at[m], send.at[m], send_sem.at[m]).wait()

    @pl.when(seg == last)
    def _():
        out_ref[...] = fin[micro - 1, pairs - 1]

        @pl.loop(0, last)
        def _(s):
            pltpu.make_async_copy(fin.at[0, 0], fin.at[0, 0], fin_sem).wait()

    @pl.when(seg != last)
    def _():
        pltpu.make_async_copy(got, got, got_sem).wait()
        out_ref[...] = got[...]


def per_device(samples, occupancy, weights, biases):
    segments, shards = lax.axis_size("segment"), lax.axis_size("width")
    shard = lax.axis_index("width")
    occ = occupancy[0]
    _, owned, per_col, order, _ = weights.shape
    rows, columns = samples.shape
    batch = BATCH
    micro = rows // batch
    share = rows // segments
    requests = owned * per_col

    named = occ.reshape(shards, requests)
    ours = named // owned == shard
    low = jnp.min(jnp.where(ours, named % owned, owned - 1), axis=1)
    high = jnp.max(jnp.where(ours, named % owned, 0), axis=1)
    table = jnp.stack([low, high], axis=1)
    table = lax.ppermute(table, "segment", [(i, (i - 1) % segments) for i in range(segments)])

    mine = lax.dynamic_slice_in_dim(named, shard, 1, 0)[0]
    source = mine // owned
    second = jnp.any(
        (source[:, None] == source[None, :]) & (mine[None, :] < mine[:, None]), axis=1
    )
    index = source * SLOTS + second.astype(jnp.int32)

    smem = pl.BlockSpec(memory_space=pltpu.SMEM)
    vmem = pl.BlockSpec(memory_space=pltpu.VMEM)
    return pl.pallas_call(
        kernel,
        out_shape=jax.ShapeDtypeStruct((share, columns), jnp.bfloat16),
        in_specs=[smem, smem, vmem, pl.BlockSpec(memory_space=pl.ANY), vmem],
        out_specs=vmem,
        scratch_shapes=[
            pltpu.VMEM((owned, per_col * order, order), jnp.bfloat16),
            pltpu.VMEM((micro, shards, SLOTS * batch, order), jnp.bfloat16),
            pltpu.VMEM((micro, shards, SLOTS * batch, order), jnp.bfloat16),
            pltpu.VMEM((shards * SLOTS, batch, order), jnp.float32),
            pltpu.VMEM((owned, batch, order), jnp.float32),
            pltpu.VMEM((micro, owned, batch, order), jnp.float32),
            pltpu.VMEM((micro, batch // share, share, columns), jnp.bfloat16),
            pltpu.VMEM((share, columns), jnp.bfloat16),
            pltpu.SemaphoreType.DMA,
            pltpu.SemaphoreType.DMA((micro,)),
            pltpu.SemaphoreType.DMA((micro,)),
            pltpu.SemaphoreType.DMA,
            pltpu.SemaphoreType.DMA,
        ],
        compiler_params=pltpu.CompilerParams(
            collective_id=0, has_side_effects=True, vmem_limit_bytes=24 * 1024 * 1024
        ),
    )(
        table.reshape(-1), index, samples,
        weights.reshape(owned, per_col * order, order), biases,
    )


def solution(mesh):
    in_specs = (
        P(None, "width"),
        P("segment", None, None),
        P("segment", "width", None, None, None),
        P("segment", "width"),
    )
    return jax.shard_map(
        per_device, mesh=mesh, in_specs=in_specs, out_specs=P("segment", "width"), check_vma=False
    )
```

```python
import jax
import jax.numpy as jnp
from jax import lax
from jax.experimental import pallas as pl
from jax.experimental.pallas import tpu as pltpu
from jax.sharding import PartitionSpec as P

BATCH = 4
CLIP = 4.0
SLOTS = 2
LANES = 128
MESH = pl.DeviceIdType.MESH


def kernel(
    occ_ref, samples_ref, weights_ref, bias_ref, out_ref,
    occ, occ_s, own, own_s, table, table_s, index, index_s,
    samples, w, bias, first, send0, send, recv, stage, act, fin, got,
    occ_sem, occ_s_sem, own_sem, table_in_sem, table_out_sem, table_s_sem, index_sem,
    samples_sem, w_sem, bias_sem, send0_sem, send_sem, recv_sem, fin_sem, got_sem,
):
    segments, shards = lax.axis_size("segment"), lax.axis_size("width")
    seg, me = lax.axis_index("segment"), lax.axis_index("width")
    last = segments - 1
    after = lax.rem(seg + 1, segments)
    before = lax.rem(seg + last, segments)
    micro, owned, batch, order = first.shape
    per_col, blocks = occ.shape
    share = got.shape[0]
    pairs = batch // share
    window = index.shape[1]
    offsets = sorted(range(shards), key=lambda o: -min(o, shards - o))

    load_occ = pltpu.make_async_copy(occ_ref, occ, occ_sem)
    load_occ_s = pltpu.make_async_copy(occ_ref, occ_s, occ_s_sem)
    load_w = pltpu.make_async_copy(weights_ref, w, w_sem)
    load_bias = pltpu.make_async_copy(bias_ref, bias, bias_sem)
    load_samples = pltpu.make_async_copy(samples_ref, samples, samples_sem)
    load_occ.start()
    load_occ_s.start()

    barrier = pltpu.get_barrier_semaphore()

    @pl.when(seg > 0)
    def _():
        for off in offsets:
            e = lax.rem(me + off, shards)
            pl.semaphore_signal(barrier, inc=1, device_id=(before, e), device_id_type=MESH)

    @pl.when(seg == 0)
    def _():
        for off in offsets:
            if off:
                e = lax.rem(me + off, shards)
                pl.semaphore_signal(barrier, inc=1, device_id=(seg, e), device_id_type=MESH)
        load_samples.start()

    @pl.when(seg < last)
    def _():
        pl.semaphore_signal(barrier, inc=1, device_id=(after, me), device_id_type=MESH)
        pl.semaphore_signal(barrier, inc=1, device_id=(last, me), device_id_type=MESH)

    load_w.start()
    load_bias.start()

    load_occ.wait()
    named = occ[...]
    ours = named // owned == me
    low = jnp.where(ours, named % owned, owned - 1)
    high = jnp.where(ours, named % owned, 0)
    low_row, high_row = low[0:1], high[0:1]
    for k in range(1, per_col):
        low_row = jnp.minimum(low_row, low[k:k + 1])
        high_row = jnp.maximum(high_row, high[k:k + 1])
    by = 1
    while by < owned:
        low_row = jnp.minimum(low_row, pltpu.roll(low_row, blocks - by, 1))
        high_row = jnp.maximum(high_row, pltpu.roll(high_row, blocks - by, 1))
        by *= 2
    own[0:1] = low_row
    own[1:2] = high_row

    @pl.when(seg == 0)
    def _():
        copy = pltpu.make_async_copy(own, own_s, own_sem)
        copy.start()
        load_samples.wait()
        rows = samples.shape[0]
        for c in range(owned):
            block = samples[:, c * order:(c + 1) * order].astype(jnp.float32)
            for m in range(rows // batch):
                first[m, c] = block[m * batch:(m + 1) * batch]
        copy.wait()

    pl.semaphore_wait(
        barrier,
        jnp.where(seg == last, 1 + last, shards + jnp.where(seg == 0, shards - 1, 1)),
    )

    send_table = pltpu.make_async_remote_copy(
        src_ref=own, dst_ref=table, send_sem=table_out_sem, recv_sem=table_in_sem,
        device_id=(before, me), device_id_type=MESH,
    )

    @pl.when(seg > 0)
    def _():
        send_table.start()

    def emit(m, off, block, tab, out, sem, to):
        d = lax.rem(me + off, shards)
        parts = [block(tab[j, d * owned]) for j in range(SLOTS)]
        out[m, d] = jnp.concatenate(parts, axis=0).astype(jnp.bfloat16)
        if to is None:
            pltpu.make_async_copy(out.at[m, d], recv.at[m, me], recv_sem.at[m]).start()
        else:
            pltpu.make_async_remote_copy(
                src_ref=out.at[m, d], dst_ref=recv.at[m, me],
                send_sem=sem.at[m], recv_sem=recv_sem.at[m],
                device_id=(to, d), device_id_type=MESH,
            ).start()

    @pl.when(seg == 0)
    def _():
        @pl.loop(0, micro)
        def _(m):
            for off in offsets:
                emit(m, off, lambda i: first[m, i], own_s, send0, send0_sem, seg if off else None)

    load_occ_s.wait()
    at = me * owned
    base = at // window * window
    x = occ[:, pl.ds(pl.multiple_of(base, window), window)]
    source = x // owned
    second = jnp.zeros_like(x)
    for k in range(per_col):
        for c in range(owned):
            q = occ_s[k, at + c]
            second = jnp.where((source == q // owned) & (x > q), 1, second)
    index[...] = source * SLOTS + second
    copy_index = pltpu.make_async_copy(index, index_s, index_sem)
    copy_index.start()

    @pl.when(seg < last)
    def _():
        pltpu.make_async_copy(table, table, table_in_sem).wait()
        copy = pltpu.make_async_copy(table, table_s, table_s_sem)
        copy.start()
        copy.wait()

    copy_index.wait()
    load_bias.wait()
    load_w.wait()

    @pl.loop(0, micro)
    def _(m):
        pltpu.make_async_copy(recv.at[m], recv.at[m], recv_sem.at[m]).wait()
        for e in range(shards):
            both = recv[m, e].astype(jnp.float32)
            for j in range(SLOTS):
                stage[e * SLOTS + j] = both[j * batch:(j + 1) * batch]
        for c in range(owned):
            picked = [stage[index_s[k, at - base + c]] for k in range(per_col)]
            picked = jnp.concatenate(picked, axis=1).astype(jnp.bfloat16)
            pre = jnp.dot(picked, w[c], preferred_element_type=jnp.float32)
            pre = pre + bias[0:1, c * order:(c + 1) * order]
            act[c] = jnp.clip(pre, 0.0, CLIP)

        @pl.when(seg < last)
        def _():
            for off in offsets:
                emit(m, off, lambda i: act[i], table_s, send, send_sem, after)

        @pl.when(seg == last)
        def _():
            for j in range(pairs):
                for c in range(owned):
                    fin[m, j, :, c * order:(c + 1) * order] = act[
                        c, j * share:(j + 1) * share, :
                    ].astype(jnp.bfloat16)
                owner = m * pairs + j

                @pl.when(owner != last)
                def _():
                    pltpu.make_async_remote_copy(
                        src_ref=fin.at[m, j], dst_ref=got,
                        send_sem=fin_sem, recv_sem=got_sem,
                        device_id=(owner, me), device_id_type=MESH,
                    ).start()

    @pl.when(seg > 0)
    def _():
        send_table.wait_send()

    @pl.when(seg == 0)
    def _():
        @pl.loop(0, micro)
        def _(m):
            sent = send0.at[m, pl.ds(0, shards - 1)]
            pltpu.make_async_copy(sent, sent, send0_sem.at[m]).wait()

    @pl.when(seg < last)
    def _():
        @pl.loop(0, micro)
        def _(m):
            pltpu.make_async_copy(send.at[m], send.at[m], send_sem.at[m]).wait()

        pltpu.make_async_copy(got, got, got_sem).wait()
        out_ref[...] = got[...]

    @pl.when(seg == last)
    def _():
        out_ref[...] = fin[micro - 1, pairs - 1]

        @pl.loop(0, last)
        def _(s):
            pltpu.make_async_copy(fin.at[0, 0], fin.at[0, 0], fin_sem).wait()


def per_device(samples, occupancy, weights, biases):
    segments, shards = lax.axis_size("segment"), lax.axis_size("width")
    _, owned, per_col, order, _ = weights.shape
    rows, columns = samples.shape
    blocks = occupancy.shape[1]
    batch = BATCH
    micro = rows // batch
    share = rows // segments
    window = min(LANES, blocks)

    hbm = pl.BlockSpec(memory_space=pltpu.HBM)
    slots = (micro, shards, SLOTS * batch, order)
    copies = pltpu.SemaphoreType.DMA
    return pl.pallas_call(
        kernel,
        out_shape=jax.ShapeDtypeStruct((share, columns), jnp.bfloat16),
        in_specs=[hbm] * 4,
        out_specs=pl.BlockSpec(memory_space=pltpu.VMEM),
        scratch_shapes=[
            pltpu.VMEM((per_col, blocks), jnp.int32),
            pltpu.SMEM((per_col, blocks), jnp.int32),
            pltpu.VMEM((SLOTS, blocks), jnp.int32),
            pltpu.SMEM((SLOTS, blocks), jnp.int32),
            pltpu.VMEM((SLOTS, blocks), jnp.int32),
            pltpu.SMEM((SLOTS, blocks), jnp.int32),
            pltpu.VMEM((per_col, window), jnp.int32),
            pltpu.SMEM((per_col, window), jnp.int32),
            pltpu.VMEM((rows, columns), jnp.bfloat16),
            pltpu.VMEM((owned, per_col * order, order), jnp.bfloat16),
            pltpu.VMEM((1, columns), jnp.float32),
            pltpu.VMEM((micro, owned, batch, order), jnp.float32),
            pltpu.VMEM(slots, jnp.bfloat16),
            pltpu.VMEM(slots, jnp.bfloat16),
            pltpu.VMEM(slots, jnp.bfloat16),
            pltpu.VMEM((shards * SLOTS, batch, order), jnp.float32),
            pltpu.VMEM((owned, batch, order), jnp.float32),
            pltpu.VMEM((micro, batch // share, share, columns), jnp.bfloat16),
            pltpu.VMEM((share, columns), jnp.bfloat16),
        ]
        + [copies] * 10
        + [copies((micro,))] * 3
        + [copies] * 2,
        compiler_params=pltpu.CompilerParams(
            collective_id=0, has_side_effects=True, vmem_limit_bytes=60 * 1024 * 1024
        ),
    )(
        jnp.transpose(occupancy[0]), samples,
        weights.reshape(owned, per_col * order, order), biases,
    )


def solution(mesh):
    in_specs = (
        P(None, "width"),
        P("segment", None, None),
        P("segment", "width", None, None, None),
        P("segment", "width"),
    )
    return jax.shard_map(
        per_device, mesh=mesh, in_specs=in_specs, out_specs=P("segment", "width"), check_vma=False
    )
```

```python
import jax
import jax.numpy as jnp
from jax import lax
from jax.experimental import pallas as pl
from jax.experimental.pallas import tpu as pltpu
from jax.sharding import PartitionSpec as P

BATCH = 2
CLIP = 4.0
SLOTS = 2
LANES = 128
MESH = pl.DeviceIdType.MESH


def kernel(
    occ_ref, samples_ref, weights_ref, bias_ref, out_ref,
    occ, occ_s, own, table, table_s, first_table, first_table_s, index, index_s,
    samples, w, bias, first, send0, send, recv, stage, act, fin, got,
    occ_sem, occ_s_sem, table_in_sem, table_out_sem, table_s_sem, first_in_sem, first_s_sem,
    index_sem, ready_sem, samples_sem, w_sem, bias_sem, send0_sem, send_sem, recv_sem, fin_sem, got_sem,
):
    segments, shards = lax.axis_size("segment"), lax.axis_size("width")
    seg, me = lax.axis_index("segment"), lax.axis_index("width")
    last = segments - 1
    feeder = segments * 3 // 4
    after = lax.rem(seg + 1, segments)
    before = lax.rem(seg + last, segments)
    micro, owned, batch, order = first.shape
    per_col, blocks = occ.shape
    share = got.shape[0]
    pairs = batch // share
    window = index.shape[1]
    offsets = sorted(range(shards), key=lambda o: -min(o, shards - o))

    load_occ = pltpu.make_async_copy(occ_ref, occ, occ_sem)
    load_occ_s = pltpu.make_async_copy(occ_ref, occ_s, occ_s_sem)
    half = owned // 2
    load_w = [
        pltpu.make_async_copy(
            weights_ref.at[pl.ds(i * half, half)], w.at[:, :, pl.ds(i * order, order)], w_sem.at[i]
        )
        for i in range(2)
    ]
    load_bias = pltpu.make_async_copy(bias_ref, bias, bias_sem)
    load_samples = pltpu.make_async_copy(samples_ref, samples, samples_sem)
    load_occ.start()
    load_occ_s.start()

    barrier = pltpu.get_barrier_semaphore()

    def signal_all(semaphore, to):
        for off in offsets:
            e = lax.rem(me + off, shards)
            pl.semaphore_signal(semaphore, inc=1, device_id=(to, e), device_id_type=MESH)

    @pl.when(seg == 0)
    def _():
        signal_all(barrier, feeder)

    @pl.when(seg == feeder)
    def _():
        pl.semaphore_signal(barrier, inc=1, device_id=(0, me), device_id_type=MESH)
        load_samples.start()

    @pl.when(seg < last)
    def _():
        signal_all(barrier, after)
        pl.semaphore_signal(barrier, inc=1, device_id=(last, me), device_id_type=MESH)

    for load in load_w:
        load.start()
    load_bias.start()

    load_occ.wait()
    named = occ[...]
    ours = named // owned == me
    low = jnp.where(ours, named % owned, owned - 1)
    high = jnp.where(ours, named % owned, 0)
    low_row, high_row = low[0:1], high[0:1]
    for k in range(1, per_col):
        low_row = jnp.minimum(low_row, low[k:k + 1])
        high_row = jnp.maximum(high_row, high[k:k + 1])
    by = 1
    while by < owned:
        low_row = jnp.minimum(low_row, pltpu.roll(low_row, blocks - by, 1))
        high_row = jnp.maximum(high_row, pltpu.roll(high_row, blocks - by, 1))
        by *= 2
    own[0:1] = low_row
    own[1:2] = high_row

    @pl.when(seg == feeder)
    def _():
        load_samples.wait()
        rows = samples.shape[0]
        for c in range(owned):
            block = samples[:, c * order:(c + 1) * order].astype(jnp.float32)
            for m in range(rows // batch):
                first[m, c] = block[m * batch:(m + 1) * batch]

    pl.semaphore_wait(
        barrier,
        jnp.where(seg == 0, 1, shards)
        + jnp.where(seg == feeder, shards, 0)
        + jnp.where(seg == last, last, 0),
    )

    send_table = pltpu.make_async_remote_copy(
        src_ref=own, dst_ref=table, send_sem=table_out_sem, recv_sem=table_in_sem,
        device_id=(before, me), device_id_type=MESH,
    )
    send_first_table = pltpu.make_async_remote_copy(
        src_ref=own, dst_ref=first_table, send_sem=table_out_sem, recv_sem=first_in_sem,
        device_id=(feeder, me), device_id_type=MESH,
    )

    @pl.when(seg == 0)
    def _():
        send_first_table.start()

    @pl.when(seg > 0)
    def _():
        send_table.start()

    def emit(m, block, tab, out, sem, to):
        for off in offsets:
            d = lax.rem(me + off, shards)
            parts = [block(tab[j, d * owned]) for j in range(SLOTS)]
            out[m, d] = jnp.concatenate(parts, axis=0).astype(jnp.bfloat16)
            pltpu.make_async_remote_copy(
                src_ref=out.at[m, d], dst_ref=recv.at[m, me],
                send_sem=sem.at[m], recv_sem=recv_sem.at[m],
                device_id=(to, d), device_id_type=MESH,
            ).start()

    @pl.when(seg == feeder)
    def _():
        pltpu.make_async_copy(first_table, first_table, first_in_sem).wait()
        copy = pltpu.make_async_copy(first_table, first_table_s, first_s_sem)
        copy.start()
        copy.wait()

        @pl.loop(0, micro)
        def _(m):
            emit(m, lambda i: first[m, i], first_table_s, send0, send0_sem, 0)

    @pl.when(seg > 0)
    def _():
        signal_all(ready_sem, before)

    load_occ_s.wait()
    at = me * owned
    base = at // window * window
    x = occ[:, pl.ds(pl.multiple_of(base, window), window)]
    source = x // owned
    second = jnp.zeros_like(x)
    for k in range(per_col):
        for c in range(owned):
            q = occ_s[k, at + c]
            second = jnp.where((source == q // owned) & (x > q), 1, second)
    index[...] = source * SLOTS + second
    copy_index = pltpu.make_async_copy(index, index_s, index_sem)
    copy_index.start()

    @pl.when(seg < last)
    def _():
        pltpu.make_async_copy(table, table, table_in_sem).wait()
        copy = pltpu.make_async_copy(table, table_s, table_s_sem)
        copy.start()
        copy.wait()
        pl.semaphore_wait(ready_sem, shards)

    copy_index.wait()
    load_bias.wait()
    for load in load_w:
        load.wait()

    @pl.loop(0, micro)
    def _(m):
        pltpu.make_async_copy(recv.at[m], recv.at[m], recv_sem.at[m]).wait()
        for e in range(shards):
            both = recv[m, e].astype(jnp.float32)
            for j in range(SLOTS):
                stage[e * SLOTS + j] = both[j * batch:(j + 1) * batch]
        for c in range(half):
            picked = [
                jnp.concatenate(
                    [stage[index_s[k, at - base + c + i * half]] for i in range(2)], axis=0
                )
                for k in range(per_col)
            ]
            picked = jnp.concatenate(picked, axis=1).astype(jnp.bfloat16)
            pre = jnp.dot(picked, w[c], preferred_element_type=jnp.float32)
            for i in range(2):
                at_c = c + i * half
                own_pre = pre[i * batch:(i + 1) * batch, i * order:(i + 1) * order]
                own_pre = own_pre + bias[0:1, at_c * order:(at_c + 1) * order]
                act[at_c] = jnp.clip(own_pre, 0.0, CLIP)

        @pl.when(seg < last)
        def _():
            emit(m, lambda i: act[i], table_s, send, send_sem, after)

        @pl.when(seg == last)
        def _():
            for j in range(pairs):
                for c in range(owned):
                    fin[m, j, :, c * order:(c + 1) * order] = act[
                        c, j * share:(j + 1) * share, :
                    ].astype(jnp.bfloat16)
                owner = m * pairs + j

                @pl.when(owner != last)
                def _():
                    pltpu.make_async_remote_copy(
                        src_ref=fin.at[m, j], dst_ref=got,
                        send_sem=fin_sem, recv_sem=got_sem,
                        device_id=(owner, me), device_id_type=MESH,
                    ).start()

    pltpu.make_async_copy(own, own, table_out_sem).wait()

    @pl.when(seg == feeder)
    def _():
        @pl.loop(0, micro)
        def _(m):
            pltpu.make_async_copy(send0.at[m], send0.at[m], send0_sem.at[m]).wait()

    @pl.when(seg < last)
    def _():
        @pl.loop(0, micro)
        def _(m):
            pltpu.make_async_copy(send.at[m], send.at[m], send_sem.at[m]).wait()

        pltpu.make_async_copy(got, got, got_sem).wait()
        out_ref[...] = got[...]

    @pl.when(seg == last)
    def _():
        out_ref[...] = fin[micro - 1, pairs - 1]

        @pl.loop(0, last)
        def _(s):
            pltpu.make_async_copy(fin.at[0, 0], fin.at[0, 0], fin_sem).wait()


def per_device(samples, occupancy, weights, biases):
    segments, shards = lax.axis_size("segment"), lax.axis_size("width")
    _, owned, per_col, order, _ = weights.shape
    rows, columns = samples.shape
    blocks = occupancy.shape[1]
    batch = BATCH
    micro = rows // batch
    share = rows // segments
    window = min(LANES, blocks)

    hbm = pl.BlockSpec(memory_space=pltpu.HBM)
    slots = (micro, shards, SLOTS * batch, order)
    copies = pltpu.SemaphoreType.DMA
    return pl.pallas_call(
        kernel,
        out_shape=jax.ShapeDtypeStruct((share, columns), jnp.bfloat16),
        in_specs=[hbm] * 4,
        out_specs=pl.BlockSpec(memory_space=pltpu.VMEM),
        scratch_shapes=[
            pltpu.VMEM((per_col, blocks), jnp.int32),
            pltpu.SMEM((per_col, blocks), jnp.int32),
            pltpu.VMEM((SLOTS, blocks), jnp.int32),
            pltpu.VMEM((SLOTS, blocks), jnp.int32),
            pltpu.SMEM((SLOTS, blocks), jnp.int32),
            pltpu.VMEM((SLOTS, blocks), jnp.int32),
            pltpu.SMEM((SLOTS, blocks), jnp.int32),
            pltpu.VMEM((per_col, window), jnp.int32),
            pltpu.SMEM((per_col, window), jnp.int32),
            pltpu.VMEM((rows, columns), jnp.bfloat16),
            pltpu.VMEM((owned // 2, per_col * order, 2 * order), jnp.bfloat16),
            pltpu.VMEM((1, columns), jnp.float32),
            pltpu.VMEM((micro, owned, batch, order), jnp.float32),
            pltpu.VMEM(slots, jnp.bfloat16),
            pltpu.VMEM(slots, jnp.bfloat16),
            pltpu.VMEM(slots, jnp.bfloat16),
            pltpu.VMEM((shards * SLOTS, batch, order), jnp.float32),
            pltpu.VMEM((owned, batch, order), jnp.float32),
            pltpu.VMEM((micro, batch // share, share, columns), jnp.bfloat16),
            pltpu.VMEM((share, columns), jnp.bfloat16),
        ]
        + [copies] * 8
        + [pltpu.SemaphoreType.REGULAR, copies]
        + [copies((2,)), copies]
        + [copies((micro,))] * 3
        + [copies] * 2,
        compiler_params=pltpu.CompilerParams(
            collective_id=0, has_side_effects=True, vmem_limit_bytes=60 * 1024 * 1024
        ),
    )(
        jnp.transpose(occupancy[0]), samples,
        weights.reshape(owned, per_col * order, order), biases,
    )


def solution(mesh):
    in_specs = (
        P(None, "width"),
        P("segment", None, None),
        P("segment", "width", None, None, None),
        P("segment", "width"),
    )
    return jax.shard_map(
        per_device, mesh=mesh, in_specs=in_specs, out_specs=P("segment", "width"), check_vma=False
    )
```

```python
import jax
import jax.numpy as jnp
from jax import lax
from jax.experimental import pallas as pl
from jax.experimental.pallas import tpu as pltpu
from jax.sharding import PartitionSpec as P

BATCH = 2
CLIP = 4.0
SLOTS = 2
GROUP = 2
HEAD = 5
LANES = 128
MESH = pl.DeviceIdType.MESH


def kernel(
    occ_ref, samples_ref, weights_ref, bias_ref, out_ref,
    occ, occ_s, own, own_s, table, table_s, first_table, first_table_s, index, index_s,
    samples, w, bias, first, send0, send, recv, stage, act, fin, got,
    occ_sem, occ_s_sem, own_sem, table_in_sem, table_out_sem, table_s_sem, first_in_sem, first_s_sem,
    index_sem, ready_sem, samples_sem, w_sem, bias_sem, send0_sem, send_sem, recv_sem, fin_sem, got_sem,
):
    segments, shards = lax.axis_size("segment"), lax.axis_size("width")
    seg, me = lax.axis_index("segment"), lax.axis_index("width")
    last = segments - 1
    feeder = segments * 3 // 4
    after = lax.rem(seg + 1, segments)
    before = lax.rem(seg + last, segments)
    micro, owned, batch, order = first.shape
    per_col, blocks = occ.shape
    share = got.shape[0]
    pairs = batch // share
    head = min(HEAD, micro)
    window = index.shape[1]
    offsets = sorted(range(shards), key=lambda o: -min(o, shards - o))

    load_occ = pltpu.make_async_copy(occ_ref, occ, occ_sem)
    load_occ_s = pltpu.make_async_copy(occ_ref, occ_s, occ_s_sem)
    load_w = pltpu.make_async_copy(weights_ref, w, w_sem)
    load_bias = pltpu.make_async_copy(bias_ref, bias, bias_sem)
    load_samples = pltpu.make_async_copy(samples_ref, samples, samples_sem)

    barrier = pltpu.get_barrier_semaphore()

    def signal_all(semaphore, to, others=False):
        for off in offsets:
            if others and off == 0:
                continue
            e = lax.rem(me + off, shards)
            pl.semaphore_signal(semaphore, inc=1, device_id=(to, e), device_id_type=MESH)

    @pl.when(seg == 0)
    def _():
        signal_all(barrier, seg, others=True)
        signal_all(barrier, feeder)
        load_samples.start()

    load_occ.start()
    load_occ_s.start()

    @pl.when(seg == feeder)
    def _():
        pl.semaphore_signal(barrier, inc=1, device_id=(0, me), device_id_type=MESH)
        load_samples.start()

    @pl.when(seg < last)
    def _():
        signal_all(barrier, after)
        pl.semaphore_signal(barrier, inc=1, device_id=(last, me), device_id_type=MESH)

    load_w.start()
    load_bias.start()

    load_occ.wait()
    named = occ[...]
    ours = named // owned == me
    low = jnp.where(ours, named % owned, owned - 1)
    high = jnp.where(ours, named % owned, 0)
    low_row, high_row = low[0:1], high[0:1]
    for k in range(1, per_col):
        low_row = jnp.minimum(low_row, low[k:k + 1])
        high_row = jnp.maximum(high_row, high[k:k + 1])
    by = 1
    while by < owned:
        low_row = jnp.minimum(low_row, pltpu.roll(low_row, blocks - by, 1))
        high_row = jnp.maximum(high_row, pltpu.roll(high_row, blocks - by, 1))
        by *= 2
    own[0:1] = low_row
    own[1:2] = high_row

    @pl.when(seg == 0)
    def _():
        pltpu.make_async_copy(own, own_s, own_sem).start()

    @pl.when((seg == 0) | (seg == feeder))
    def _():
        load_samples.wait()
        rows = samples.shape[0]
        for c in range(owned):
            block = samples[:, c * order:(c + 1) * order].astype(jnp.float32)
            for m in range(rows // batch):
                first[m, c] = block[m * batch:(m + 1) * batch]

    @pl.when(seg == 0)
    def _():
        pltpu.make_async_copy(own, own_s, own_sem).wait()

    pl.semaphore_wait(
        barrier,
        shards
        + jnp.where(seg == feeder, shards, 0)
        + jnp.where(seg == last, last, 0),
    )

    send_table = pltpu.make_async_remote_copy(
        src_ref=own, dst_ref=table, send_sem=table_out_sem, recv_sem=table_in_sem,
        device_id=(before, me), device_id_type=MESH,
    )
    send_first_table = pltpu.make_async_remote_copy(
        src_ref=own, dst_ref=first_table, send_sem=table_out_sem, recv_sem=first_in_sem,
        device_id=(feeder, me), device_id_type=MESH,
    )

    @pl.when(seg == 0)
    def _():
        send_first_table.start()

    @pl.when(seg > 0)
    def _():
        send_table.start()

    def emit(m, block, tab, out, sem, to, to_self=False):
        for off in offsets:
            d = lax.rem(me + off, shards)
            parts = [block(tab[j, d * owned]) for j in range(SLOTS)]
            out[m, d] = jnp.concatenate(parts, axis=0).astype(jnp.bfloat16)
            if to_self and off == 0:
                pltpu.make_async_copy(out.at[m, d], recv.at[m, me], recv_sem.at[m]).start()
                continue
            pltpu.make_async_remote_copy(
                src_ref=out.at[m, d], dst_ref=recv.at[m, me],
                send_sem=sem.at[m], recv_sem=recv_sem.at[m],
                device_id=(to, d), device_id_type=MESH,
            ).start()

    @pl.when(seg == 0)
    def _():
        @pl.loop(0, head)
        def _(m):
            emit(m, lambda i: first[m, i], own_s, send0, send0_sem, seg, to_self=True)

    @pl.when(seg == feeder)
    def _():
        pltpu.make_async_copy(first_table, first_table, first_in_sem).wait()
        copy = pltpu.make_async_copy(first_table, first_table_s, first_s_sem)
        copy.start()
        copy.wait()

        @pl.loop(head, micro)
        def _(m):
            emit(m, lambda i: first[m, i], first_table_s, send0, send0_sem, 0)

    @pl.when(seg > 0)
    def _():
        signal_all(ready_sem, before)

    load_occ_s.wait()
    at = me * owned
    base = at // window * window
    x = occ[:, pl.ds(pl.multiple_of(base, window), window)]
    source = x // owned
    second = jnp.zeros_like(x)
    for k in range(per_col):
        for c in range(owned):
            q = occ_s[k, at + c]
            second = jnp.where((source == q // owned) & (x > q), 1, second)
    index[...] = source * SLOTS + second
    copy_index = pltpu.make_async_copy(index, index_s, index_sem)
    copy_index.start()

    @pl.when(seg < last)
    def _():
        pltpu.make_async_copy(table, table, table_in_sem).wait()
        copy = pltpu.make_async_copy(table, table_s, table_s_sem)
        copy.start()
        copy.wait()
        pl.semaphore_wait(ready_sem, shards)

    copy_index.wait()
    load_bias.wait()
    load_w.wait()

    @pl.loop(0, micro)
    def _(m):
        pltpu.make_async_copy(recv.at[m], recv.at[m], recv_sem.at[m]).wait()
        for e in range(shards):
            both = recv[m, e].astype(jnp.float32)
            for j in range(SLOTS):
                stage[e * SLOTS + j] = both[j * batch:(j + 1) * batch]
        for c in range(0, owned, GROUP):
            picked = [
                jnp.concatenate(
                    [stage[index_s[k, at - base + c + i]] for i in range(GROUP)], axis=0
                )
                for k in range(per_col)
            ]
            picked = jnp.concatenate(picked, axis=1).astype(jnp.bfloat16)
            wide = jnp.concatenate([w[c + i] for i in range(GROUP)], axis=1)
            pre = jnp.dot(picked, wide, preferred_element_type=jnp.float32)
            for i in range(GROUP):
                own_pre = pre[i * batch:(i + 1) * batch, i * order:(i + 1) * order]
                own_pre = own_pre + bias[0:1, (c + i) * order:(c + i + 1) * order]
                act[c + i] = jnp.clip(own_pre, 0.0, CLIP)

        @pl.when(seg < last)
        def _():
            emit(m, lambda i: act[i], table_s, send, send_sem, after)

        @pl.when(seg == last)
        def _():
            for j in range(pairs):
                for c in range(owned):
                    fin[m, j, :, c * order:(c + 1) * order] = act[
                        c, j * share:(j + 1) * share, :
                    ].astype(jnp.bfloat16)
                owner = m * pairs + j

                @pl.when(owner != last)
                def _():
                    pltpu.make_async_remote_copy(
                        src_ref=fin.at[m, j], dst_ref=got,
                        send_sem=fin_sem, recv_sem=got_sem,
                        device_id=(owner, me), device_id_type=MESH,
                    ).start()

    pltpu.make_async_copy(own, own, table_out_sem).wait()

    @pl.when(seg == 0)
    def _():
        @pl.loop(0, head)
        def _(m):
            sent = send0.at[m, pl.ds(0, shards - 1)]
            pltpu.make_async_copy(sent, sent, send0_sem.at[m]).wait()

    @pl.when(seg == feeder)
    def _():
        @pl.loop(head, micro)
        def _(m):
            pltpu.make_async_copy(send0.at[m], send0.at[m], send0_sem.at[m]).wait()

    @pl.when(seg < last)
    def _():
        @pl.loop(0, micro)
        def _(m):
            pltpu.make_async_copy(send.at[m], send.at[m], send_sem.at[m]).wait()

        pltpu.make_async_copy(got, got, got_sem).wait()
        out_ref[...] = got[...]

    @pl.when(seg == last)
    def _():
        out_ref[...] = fin[micro - 1, pairs - 1]

        @pl.loop(0, last)
        def _(s):
            pltpu.make_async_copy(fin.at[0, 0], fin.at[0, 0], fin_sem).wait()


def per_device(samples, occupancy, weights, biases):
    segments, shards = lax.axis_size("segment"), lax.axis_size("width")
    _, owned, per_col, order, _ = weights.shape
    rows, columns = samples.shape
    blocks = occupancy.shape[1]
    batch = BATCH
    micro = rows // batch
    share = rows // segments
    window = min(LANES, blocks)

    hbm = pl.BlockSpec(memory_space=pltpu.HBM)
    slots = (micro, shards, SLOTS * batch, order)
    copies = pltpu.SemaphoreType.DMA
    return pl.pallas_call(
        kernel,
        out_shape=jax.ShapeDtypeStruct((share, columns), jnp.bfloat16),
        in_specs=[hbm] * 4,
        out_specs=pl.BlockSpec(memory_space=pltpu.VMEM),
        scratch_shapes=[
            pltpu.VMEM((per_col, blocks), jnp.int32),
            pltpu.SMEM((per_col, blocks), jnp.int32),
            pltpu.VMEM((SLOTS, blocks), jnp.int32),
            pltpu.SMEM((SLOTS, blocks), jnp.int32),
            pltpu.VMEM((SLOTS, blocks), jnp.int32),
            pltpu.SMEM((SLOTS, blocks), jnp.int32),
            pltpu.VMEM((SLOTS, blocks), jnp.int32),
            pltpu.SMEM((SLOTS, blocks), jnp.int32),
            pltpu.VMEM((per_col, window), jnp.int32),
            pltpu.SMEM((per_col, window), jnp.int32),
            pltpu.VMEM((rows, columns), jnp.bfloat16),
            pltpu.VMEM((owned, per_col * order, order), jnp.bfloat16),
            pltpu.VMEM((1, columns), jnp.float32),
            pltpu.VMEM((micro, owned, batch, order), jnp.float32),
            pltpu.VMEM(slots, jnp.bfloat16),
            pltpu.VMEM(slots, jnp.bfloat16),
            pltpu.VMEM(slots, jnp.bfloat16),
            pltpu.VMEM((shards * SLOTS, batch, order), jnp.float32),
            pltpu.VMEM((owned, batch, order), jnp.float32),
            pltpu.VMEM((micro, batch // share, share, columns), jnp.bfloat16),
            pltpu.VMEM((share, columns), jnp.bfloat16),
        ]
        + [copies] * 9
        + [pltpu.SemaphoreType.REGULAR, copies]
        + [copies, copies]
        + [copies((micro,))] * 3
        + [copies] * 2,
        compiler_params=pltpu.CompilerParams(
            collective_id=0, has_side_effects=True, vmem_limit_bytes=60 * 1024 * 1024
        ),
    )(
        jnp.transpose(occupancy[0]), samples,
        weights.reshape(owned, per_col * order, order), biases,
    )


def solution(mesh):
    in_specs = (
        P(None, "width"),
        P("segment", None, None),
        P("segment", "width", None, None, None),
        P("segment", "width"),
    )
    return jax.shard_map(
        per_device, mesh=mesh, in_specs=in_specs, out_specs=P("segment", "width"), check_vma=False
    )
```

```python
import jax
import jax.numpy as jnp
from jax import lax
from jax.experimental import pallas as pl
from jax.experimental.pallas import tpu as pltpu
from jax.sharding import PartitionSpec as P

BATCH = 2
CLIP = 4.0
SLOTS = 2
GROUP = 2
HEAD = 5
LANES = 128
MESH = pl.DeviceIdType.MESH


def kernel(
    occ_ref, samples_ref, weights_ref, bias_ref, out_ref,
    occ, occ_s, own, own_s, table, table_s, first_table, first_table_s, index, index_s,
    samples, w, bias, first, send0, send, recv, stage, act, fin, got,
    occ_sem, occ_s_sem, own_sem, table_in_sem, table_out_sem, table_s_sem, first_in_sem, first_s_sem,
    index_sem, ready_sem, samples_sem, w_sem, bias_sem, send0_sem, send_sem, recv_sem, fin_sem, got_sem,
):
    segments, shards = lax.axis_size("segment"), lax.axis_size("width")
    seg, me = lax.axis_index("segment"), lax.axis_index("width")
    last = segments - 1
    feeder = segments * 3 // 4
    after = lax.rem(seg + 1, segments)
    before = lax.rem(seg + last, segments)
    micro, owned, batch, order = first.shape
    per_col, blocks = occ.shape
    share = got.shape[0]
    pairs = batch // share
    head = min(HEAD, micro)
    window = index.shape[1]
    def around(place):
        return jnp.where(place >= shards, place - shards, place)

    offsets = sorted(range(shards), key=lambda o: -min(o, shards - o))

    load_occ = pltpu.make_async_copy(occ_ref, occ, occ_sem)
    load_occ_s = pltpu.make_async_copy(occ_ref, occ_s, occ_s_sem)
    load_w = pltpu.make_async_copy(weights_ref, w, w_sem)
    load_bias = pltpu.make_async_copy(bias_ref, bias, bias_sem)
    load_samples = pltpu.make_async_copy(samples_ref, samples, samples_sem)

    barrier = pltpu.get_barrier_semaphore()

    def signal_all(semaphore, to, others=False):
        for off in offsets:
            if others and off == 0:
                continue
            e = around(me + off)
            pl.semaphore_signal(semaphore, inc=1, device_id=(to, e), device_id_type=MESH)

    @pl.when(seg == 0)
    def _():
        signal_all(barrier, seg, others=True)
        signal_all(barrier, feeder)
        load_samples.start()

    load_occ.start()
    load_occ_s.start()

    @pl.when(seg == feeder)
    def _():
        pl.semaphore_signal(barrier, inc=1, device_id=(0, me), device_id_type=MESH)
        load_samples.start()

    @pl.when(seg < last)
    def _():
        signal_all(barrier, after)
        pl.semaphore_signal(barrier, inc=1, device_id=(last, me), device_id_type=MESH)

    load_w.start()
    load_bias.start()

    load_occ.wait()
    named = occ[...]
    ours = named // owned == me
    low = jnp.where(ours, named % owned, owned - 1)
    high = jnp.where(ours, named % owned, 0)
    low_row, high_row = low[0:1], high[0:1]
    for k in range(1, per_col):
        low_row = jnp.minimum(low_row, low[k:k + 1])
        high_row = jnp.maximum(high_row, high[k:k + 1])
    by = 1
    while by < owned:
        low_row = jnp.minimum(low_row, pltpu.roll(low_row, blocks - by, 1))
        high_row = jnp.maximum(high_row, pltpu.roll(high_row, blocks - by, 1))
        by *= 2
    own[0:1] = low_row
    own[1:2] = high_row

    @pl.when(seg == 0)
    def _():
        pltpu.make_async_copy(own, own_s, own_sem).start()

    @pl.when((seg == 0) | (seg == feeder))
    def _():
        load_samples.wait()
        rows = samples.shape[0]
        for c in range(owned):
            block = samples[:, c * order:(c + 1) * order].astype(jnp.float32)
            for m in range(rows // batch):
                first[m, c] = block[m * batch:(m + 1) * batch]

    @pl.when(seg == 0)
    def _():
        pltpu.make_async_copy(own, own_s, own_sem).wait()

    pl.semaphore_wait(
        barrier,
        shards
        + jnp.where(seg == feeder, shards, 0)
        + jnp.where(seg == last, last, 0),
    )

    send_table = pltpu.make_async_remote_copy(
        src_ref=own, dst_ref=table, send_sem=table_out_sem, recv_sem=table_in_sem,
        device_id=(before, me), device_id_type=MESH,
    )
    send_first_table = pltpu.make_async_remote_copy(
        src_ref=own, dst_ref=first_table, send_sem=table_out_sem, recv_sem=first_in_sem,
        device_id=(feeder, me), device_id_type=MESH,
    )

    @pl.when(seg == 0)
    def _():
        send_first_table.start()

    @pl.when(seg > 0)
    def _():
        send_table.start()

    def emit(m, block, tab, out, sem, to, to_self=False):
        for off in offsets:
            d = around(me + off)
            parts = [block(tab[j, d * owned]) for j in range(SLOTS)]
            out[m, d] = jnp.concatenate(parts, axis=0).astype(jnp.bfloat16)
            if to_self and off == 0:
                pltpu.make_async_copy(out.at[m, d], recv.at[m, me], recv_sem.at[m]).start()
                continue
            pltpu.make_async_remote_copy(
                src_ref=out.at[m, d], dst_ref=recv.at[m, me],
                send_sem=sem.at[m], recv_sem=recv_sem.at[m],
                device_id=(to, d), device_id_type=MESH,
            ).start()

    @pl.when(seg == 0)
    def _():
        @pl.loop(0, head)
        def _(m):
            emit(m, lambda i: first[m, i], own_s, send0, send0_sem, seg, to_self=True)

    @pl.when(seg == feeder)
    def _():
        pltpu.make_async_copy(first_table, first_table, first_in_sem).wait()
        copy = pltpu.make_async_copy(first_table, first_table_s, first_s_sem)
        copy.start()
        copy.wait()

        @pl.loop(head, micro)
        def _(m):
            emit(m, lambda i: first[m, i], first_table_s, send0, send0_sem, 0)

    @pl.when(seg > 0)
    def _():
        signal_all(ready_sem, before)

    load_occ_s.wait()
    at = me * owned
    base = at // window * window
    x = occ[:, pl.ds(pl.multiple_of(base, window), window)]
    source = x // owned
    second = jnp.zeros_like(x)
    for k in range(per_col):
        for c in range(owned):
            q = occ_s[k, at + c]
            second = jnp.where((source == q // owned) & (x > q), 1, second)
    index[...] = source * SLOTS + second
    copy_index = pltpu.make_async_copy(index, index_s, index_sem)
    copy_index.start()

    @pl.when(seg < last)
    def _():
        pltpu.make_async_copy(table, table, table_in_sem).wait()
        copy = pltpu.make_async_copy(table, table_s, table_s_sem)
        copy.start()
        copy.wait()
        pl.semaphore_wait(ready_sem, shards)

    copy_index.wait()
    load_bias.wait()
    load_w.wait()

    @pl.loop(0, micro)
    def _(m):
        pltpu.make_async_copy(recv.at[m], recv.at[m], recv_sem.at[m]).wait()
        for e in range(shards):
            both = recv[m, e].astype(jnp.float32)
            for j in range(SLOTS):
                stage[e * SLOTS + j] = both[j * batch:(j + 1) * batch]
        for c in range(0, owned, GROUP):
            picked = [
                jnp.concatenate(
                    [stage[index_s[k, at - base + c + i]] for i in range(GROUP)], axis=0
                )
                for k in range(per_col)
            ]
            picked = jnp.concatenate(picked, axis=1).astype(jnp.bfloat16)
            wide = jnp.concatenate([w[c + i] for i in range(GROUP)], axis=1)
            pre = jnp.dot(picked, wide, preferred_element_type=jnp.float32)
            for i in range(GROUP):
                own_pre = pre[i * batch:(i + 1) * batch, i * order:(i + 1) * order]
                own_pre = own_pre + bias[0:1, (c + i) * order:(c + i + 1) * order]
                act[c + i] = jnp.clip(own_pre, 0.0, CLIP)

        @pl.when(seg < last)
        def _():
            emit(m, lambda i: act[i], table_s, send, send_sem, after)

        @pl.when(seg == last)
        def _():
            for j in range(pairs):
                for c in range(owned):
                    fin[m, j, :, c * order:(c + 1) * order] = act[
                        c, j * share:(j + 1) * share, :
                    ].astype(jnp.bfloat16)
                owner = m * pairs + j

                @pl.when(owner != last)
                def _():
                    pltpu.make_async_remote_copy(
                        src_ref=fin.at[m, j], dst_ref=got,
                        send_sem=fin_sem, recv_sem=got_sem,
                        device_id=(owner, me), device_id_type=MESH,
                    ).start()

    pltpu.make_async_copy(own, own, table_out_sem).wait()

    @pl.when(seg == 0)
    def _():
        @pl.loop(0, head)
        def _(m):
            sent = send0.at[m, pl.ds(0, shards - 1)]
            pltpu.make_async_copy(sent, sent, send0_sem.at[m]).wait()

    @pl.when(seg == feeder)
    def _():
        @pl.loop(head, micro)
        def _(m):
            pltpu.make_async_copy(send0.at[m], send0.at[m], send0_sem.at[m]).wait()

    @pl.when(seg < last)
    def _():
        @pl.loop(0, micro)
        def _(m):
            pltpu.make_async_copy(send.at[m], send.at[m], send_sem.at[m]).wait()

        pltpu.make_async_copy(got, got, got_sem).wait()
        out_ref[...] = got[...]

    @pl.when(seg == last)
    def _():
        out_ref[...] = fin[micro - 1, pairs - 1]

        @pl.loop(0, last)
        def _(s):
            pltpu.make_async_copy(fin.at[0, 0], fin.at[0, 0], fin_sem).wait()


def per_device(samples, occupancy, weights, biases):
    segments, shards = lax.axis_size("segment"), lax.axis_size("width")
    _, owned, per_col, order, _ = weights.shape
    rows, columns = samples.shape
    blocks = occupancy.shape[1]
    batch = BATCH
    micro = rows // batch
    share = rows // segments
    window = min(LANES, blocks)

    hbm = pl.BlockSpec(memory_space=pltpu.HBM)
    slots = (micro, shards, SLOTS * batch, order)
    copies = pltpu.SemaphoreType.DMA
    return pl.pallas_call(
        kernel,
        out_shape=jax.ShapeDtypeStruct((share, columns), jnp.bfloat16),
        in_specs=[hbm] * 4,
        out_specs=pl.BlockSpec(memory_space=pltpu.VMEM),
        scratch_shapes=[
            pltpu.VMEM((per_col, blocks), jnp.int32),
            pltpu.SMEM((per_col, blocks), jnp.int32),
            pltpu.VMEM((SLOTS, blocks), jnp.int32),
            pltpu.SMEM((SLOTS, blocks), jnp.int32),
            pltpu.VMEM((SLOTS, blocks), jnp.int32),
            pltpu.SMEM((SLOTS, blocks), jnp.int32),
            pltpu.VMEM((SLOTS, blocks), jnp.int32),
            pltpu.SMEM((SLOTS, blocks), jnp.int32),
            pltpu.VMEM((per_col, window), jnp.int32),
            pltpu.SMEM((per_col, window), jnp.int32),
            pltpu.VMEM((rows, columns), jnp.bfloat16),
            pltpu.VMEM((owned, per_col * order, order), jnp.bfloat16),
            pltpu.VMEM((1, columns), jnp.float32),
            pltpu.VMEM((micro, owned, batch, order), jnp.float32),
            pltpu.VMEM(slots, jnp.bfloat16),
            pltpu.VMEM(slots, jnp.bfloat16),
            pltpu.VMEM(slots, jnp.bfloat16),
            pltpu.VMEM((shards * SLOTS, batch, order), jnp.float32),
            pltpu.VMEM((owned, batch, order), jnp.float32),
            pltpu.VMEM((micro, batch // share, share, columns), jnp.bfloat16),
            pltpu.VMEM((share, columns), jnp.bfloat16),
        ]
        + [copies] * 9
        + [pltpu.SemaphoreType.REGULAR, copies]
        + [copies, copies]
        + [copies((micro,))] * 3
        + [copies] * 2,
        compiler_params=pltpu.CompilerParams(
            collective_id=0, has_side_effects=True, vmem_limit_bytes=60 * 1024 * 1024
        ),
    )(
        jnp.transpose(occupancy[0]), samples,
        weights.reshape(owned, per_col * order, order), biases,
    )


def solution(mesh):
    in_specs = (
        P(None, "width"),
        P("segment", None, None),
        P("segment", "width", None, None, None),
        P("segment", "width"),
    )
    return jax.shard_map(
        per_device, mesh=mesh, in_specs=in_specs, out_specs=P("segment", "width"), check_vma=False
    )
```
